32 devices in a mesh: expert: 16 (over z, y, x), hidden: 2 (over core).
Axes of the slice: x: 2, y: 2, z: 4, core: 2. Of those that a mesh axis runs over, the one named last changes fastest.
Arguments:
- tokens: bfloat16 [1024, 4096], P('expert', 'hidden'), may hold values from -6 to 6
- route_ids: int32 [1024, 8], P('expert'), may hold values from 0 to 15, all different within a row; in each aligned block of 64 rows (0 to 63, 64 to 127, ...) at most 48 rows name the same one
- route_weights: float32 [1024, 8], P('expert'), may hold values from 0.05 to 1
- gate_up: bfloat16 [16, 2, 768, 4096], P('expert', None, 'hidden'), may hold values from -0.09375 to 0.09375
- down_proj: bfloat16 [16, 768, 4096], P('expert', None, 'hidden'), may hold values from -0.21875 to 0.21875
Outputs:
- layer_out: bfloat16 [1024, 4096], P('expert', 'hidden')
- hessian: float32 [16, 768, 768], P('expert', 'hidden')
The draws below stay inside these ranges and needn't reach their ends.
Inputs may be any that keep to these rules, and one draw needn't show every extreme that they name: `route_ids`: each token names 8 different experts. Within the rows of one device (aligned blocks of 64 tokens) no expert is named more than 48 times, and in some block one expert is named exactly 48 times. Every expert is named by some token.
All inputs are finite; a program needn't handle non-finite values.
Results may differ from the reference program's by a relative error of at most 0.012.
Values may be sent and summed in bfloat16 or wider, within the bound.
A program may use at most 64 MiB of HBM per device.

```python
import math
import jax
import jax.numpy as jnp
import numpy as np
from jax import lax

D = 4096
FF = 768
TOP = 8
TOK_DEV = 64
EXPERTS = 16
TOKENS = 1024
CAP = 48
N_EXPERT = 16


def block_levels(rng, shape, pieces, smallest, largest):
    def one(dim, blocks):
        draws = jax.random.uniform(jax.random.fold_in(jax.random.fold_in(rng, 6), dim), (blocks,), jnp.float32, smallest / len(pieces), largest / len(pieces))
        return jnp.repeat(jnp.exp(draws), shape[dim] // blocks).reshape((-1,) + (1,) * (len(shape) - dim - 1))

    gain = one(*pieces[0])
    for cut in pieces[1:]:
        gain = gain * one(*cut)
    return gain


def deal_out(stream_key, own, number, rows, number_of, top, limit, skew):
    ranking = jax.random.permutation(stream_key, number_of)
    crowded, usual = shares(number_of, rows * top, limit, skew, True), shares(number_of, rows * top, limit, skew, False)
    places = jnp.arange(number_of)

    def named(tallies, offset_by):
        used = int((tallies > 0).sum())
        fixed = max(1, used // 4)
        passed = fixed + (places - fixed + offset_by * (used - fixed)) % max(1, number_of - fixed)
        return jnp.zeros((number_of,), jnp.int32).at[ranking[jnp.where(places < fixed, places, passed)]].set(jnp.asarray(tallies, jnp.int32))

    tallies = jnp.where(number % 4 == 0, named(crowded, number // 4), named(usual, number - number // 4 - 1))
    mixed = jax.random.permutation(jax.random.fold_in(own, 3), number_of)
    donor, taker = mixed[0:number_of // 2 * 2:2], mixed[1:number_of // 2 * 2:2]
    slack = jnp.minimum(tallies[donor] - 1, limit - tallies[taker]) // 2
    slack = jnp.where((donor == ranking[0]) | (taker == ranking[0]) | (tallies[taker] == 0), 0, jnp.maximum(slack, 0))
    passed = jax.random.randint(jax.random.fold_in(own, 4), (number_of // 2,), 0, 1 << 20) % (slack + 1)
    tallies = tallies.at[donor].add(-passed).at[taker].add(passed)
    labels = jnp.searchsorted(jnp.cumsum(tallies), jnp.arange(rows * top), side="right").astype(jnp.int32)
    listing = labels.reshape(top, rows).T
    listing = listing[jax.random.permutation(jax.random.fold_in(own, 1), rows)]
    offset_by = jax.random.randint(jax.random.fold_in(own, 2), (rows, 1), 0, top)
    return jnp.take_along_axis(listing, (jnp.arange(top)[None, :] + offset_by) % top, axis=1)


def shares(amount, total, limit, skew, full):
    weights = [(1 << 20) // math.isqrt(rank ** skew) + 1 for rank in range(1, amount + 1)]
    largest = limit if full else min(limit, max(-(-total // amount), total * weights[0] // sum(weights)))
    least = 1 if total - largest >= amount - 1 else 0
    counts, spare = [largest] + [least] * (amount - 1), total - largest - least * (amount - 1)
    while spare > 0:
        movable = [i for i in range(1, amount) if counts[i] < largest] or [i for i in range(1, amount) if counts[i] < limit]
        whole, remaining = sum([weights[i] for i in movable]), spare
        for i in movable:
            addition = min(limit - counts[i], max(1, remaining * weights[i] // whole), spare)
            counts[i] = counts[i] + addition
            spare = spare - addition
    return np.array(counts)


def gaussian(key, extent, deviation, bound, split=(), kind=jnp.bfloat16):
    level = block_levels(key, extent, split, -0.22, 0.18) if split else 1.0
    drawn = jax.random.normal(key, extent, jnp.float32) * deviation * level
    return jnp.minimum(jnp.maximum(drawn, -bound), bound).astype(kind)


def setup_inputs(seed: int = 0) -> dict:
    key_of = jax.random.split(jax.random.key(seed), 6)
    tokens = gaussian(key_of[0], (TOKENS, D), 1.0, 6.0, ((0, 16), (1, 2)))
    route_ids_keys = jax.random.split(jax.random.fold_in(key_of[1], 1), TOKENS // TOK_DEV)
    route_ids_turns = jax.random.permutation(jax.random.fold_in(key_of[1], 3), TOKENS // TOK_DEV)
    route_ids = jax.vmap(lambda own, number: deal_out(jax.random.fold_in(key_of[1], 2), own, number, TOK_DEV, EXPERTS, TOP, CAP, 2))(route_ids_keys, route_ids_turns).reshape((TOKENS, TOP))
    route_weights = jnp.clip(jnp.exp(math.log(1.0) - 2.9957323 * jax.random.uniform(key_of[2], (TOKENS, TOP), jnp.float32) ** block_levels(key_of[2], (TOKENS, TOP), ((0, 16),), -0.2, 0.2)), 0.05, 1.0)
    gate_up = gaussian(key_of[3], (EXPERTS, 2, FF, D), D ** -0.5, 0.09375, ((0, 16), (2, 2)))
    down_proj = gaussian(key_of[4], (EXPERTS, FF, D), FF ** -0.5, 0.21875, ((0, 16), (2, 2)))
    return {"tokens": tokens, "route_ids": route_ids, "route_weights": route_weights, "gate_up": gate_up, "down_proj": down_proj}


def reference(tokens, route_ids, route_weights, gate_up, down_proj):
    slots_all = N_EXPERT * CAP
    flat_ids = route_ids.reshape(-1).astype(jnp.int32)
    route_share = route_weights / jnp.sum(route_weights, axis=1, keepdims=True)
    flat_share = route_share.reshape(-1)
    positions = jnp.arange(slots_all, dtype=jnp.int32)

    def one_expert(layer_acc, inputs):
        expert, weight_pair, weight_down = inputs
        chosen = flat_ids == expert
        number = jnp.sum(chosen.astype(jnp.int32))
        routes = jnp.nonzero(chosen, size=slots_all, fill_value=0)[0].astype(jnp.int32)
        live_rows = positions < number
        token_rows = (routes // TOP).astype(jnp.int32)
        gathered = jnp.where(live_rows[:, None], tokens[token_rows], jnp.zeros((), jnp.bfloat16))
        gate_val = jnp.dot(gathered, weight_pair[0].T, preferred_element_type=jnp.float32)
        upward = jnp.dot(gathered, weight_pair[1].T, preferred_element_type=jnp.float32)
        hidden = (jax.nn.silu(gate_val) * upward).astype(jnp.bfloat16)
        gram_block = jnp.dot(hidden.T, hidden, preferred_element_type=jnp.float32) * (2.0 / number.astype(jnp.float32))
        expert_out = jnp.dot(hidden, weight_down, preferred_element_type=jnp.float32).astype(jnp.bfloat16)
        weights_live = jnp.where(live_rows, flat_share[routes], 0.0)
        contrib = weights_live[:, None] * expert_out.astype(jnp.float32)
        layer_acc = layer_acc.at[token_rows].add(contrib)
        return layer_acc, gram_block

    start_acc = jnp.zeros((tokens.shape[0], tokens.shape[1]), jnp.float32)
    experts_idx = jnp.arange(EXPERTS, dtype=jnp.int32)
    layer_acc, hessian = lax.scan(one_expert, start_acc, (experts_idx, gate_up, down_proj))
    return layer_acc.astype(jnp.bfloat16), hessian
```

```python
import jax
import jax.numpy as jnp
from jax import lax
from jax.sharding import PartitionSpec as P


def body(tokens, route_ids, route_weights, gate_up, down_proj):
    local_experts = gate_up.shape[0]
    all_experts = local_experts * lax.axis_size("expert")
    share = route_weights / jnp.sum(route_weights, axis=1, keepdims=True)
    hit = route_ids[:, :, None] == jnp.arange(all_experts, dtype=jnp.int32)[None, None, :]
    table = jnp.sum(jnp.where(hit, share[:, :, None], 0.0), axis=1)
    table = lax.all_gather(table.T, "expert", axis=1, tiled=True)
    mine = lax.dynamic_slice_in_dim(
        table, lax.axis_index("expert") * local_experts, local_experts, axis=0
    )
    features = lax.all_gather(tokens, "expert", axis=0, tiled=True)
    features = lax.all_gather(features, "hidden", axis=1, tiled=True)
    routed = jnp.sum((mine > 0).astype(jnp.float32), axis=1)
    gate = jnp.einsum("td,efd->etf", features, gate_up[:, 0], preferred_element_type=jnp.float32)
    upward = jnp.einsum("td,efd->etf", features, gate_up[:, 1], preferred_element_type=jnp.float32)
    hidden = jnp.where((mine > 0)[:, :, None], jax.nn.silu(gate) * upward, 0.0).astype(jnp.bfloat16)
    rows = lax.all_gather(hidden, "hidden", axis=2, tiled=True)
    columns = jnp.einsum("etf,etg->efg", hidden, rows, preferred_element_type=jnp.float32)
    hessian = columns * (2.0 / routed)[:, None, None]
    out = jnp.einsum("etg,egd->etd", rows, down_proj, preferred_element_type=jnp.float32)
    out = jnp.sum(out * mine[:, :, None], axis=0).astype(jnp.bfloat16)
    layer_out = lax.psum_scatter(out, "expert", scatter_dimension=0, tiled=True)
    return (layer_out, hessian)


def solution(mesh):
    return jax.shard_map(
        body,
        mesh=mesh,
        in_specs=(
            P("expert", "hidden"),
            P("expert", None),
            P("expert", None),
            P("expert", None, "hidden", None),
            P("expert", None, "hidden"),
        ),
        out_specs=(P("expert", "hidden"), P("expert", "hidden", None)),
        check_vma=False,
    )
```

```python
import jax
import jax.numpy as jnp
from jax import lax
from jax.experimental import pallas as pl
from jax.experimental.pallas import tpu as pltpu
from jax.sharding import PartitionSpec as P

PLANES = 4
PLANE = 4
FIRST = (1, 2, 1, 2)
SECOND = (2, 0, 3, 1)
THIRD = (3, 3, 0, 0)
NAMES = ("zr", "xr", "yr", "dx", "dy", "c0", "c1", "c2", "c3", "tz", "tx", "ty", "td", "hr",
         "ax", "ay", "bx0", "bx1", "by0", "by1", "z0", "z1")
SENDS = 128


def pick(values, z):
    chosen = jnp.int32(values[0])
    for place in range(1, len(values)):
        chosen = jnp.where(z == place, jnp.int32(values[place]), chosen)
    return chosen


def layer_kernel(tokens, table, gate_up, down, out, hess,
                 feats, shares, hid, part, got_ax, got_ay, got_bx, got_by, got_z,
                 w_gate, w_down, send_sem, recv_sem, load_sem):
    rows, width = tokens.shape
    half = rows // 2
    units = hid.shape[-1]
    me = lax.axis_index("expert")
    c = lax.axis_index("hidden")
    z, j = me // PLANE, me % PLANE
    xj, yj, dj = j + 1 - 2 * (j % 2), (j + 2) % PLANE, PLANE - 1 - j
    ex, ey = z * PLANE + xj, z * PLANE + yj
    at_end = z % (PLANES - 1) == 0
    inside = z % (PLANES - 1) != 0
    a1, a2, a3 = pick(FIRST, z), pick(SECOND, z), pick(THIRD, z)
    order = (z, a1, a3, a2)
    lo, hi = pl.ds(0, half), pl.ds(half, half)
    all_rows = pl.ds(0, rows)
    started = []

    load_gate = pltpu.make_async_copy(gate_up.at[0], w_gate, load_sem.at[0])
    load_down = pltpu.make_async_copy(down.at[0], w_down, load_sem.at[1])
    load_gate.start()
    load_down.start()

    def sem(name, k):
        return recv_sem.at[NAMES.index(name) * PLANES + k]

    def send(src, dst, to, name, k, core=None, when=None):
        copy = pltpu.make_async_remote_copy(
            src_ref=src, dst_ref=dst, send_sem=send_sem.at[len(started)], recv_sem=sem(name, k),
            device_id=(to, c if core is None else core), device_id_type=pl.DeviceIdType.MESH)
        started.append((copy, when))
        if when is None:
            copy.start()
        else:
            pl.when(when)(copy.start)

    def landed(dst, name, k):
        pltpu.make_async_remote_copy(
            src_ref=dst, dst_ref=dst, send_sem=send_sem.at[0], recv_sem=sem(name, k),
            device_id=(me, 1 - c), device_id_type=pl.DeviceIdType.MESH).wait_recv()

    def block(k, q, part_rows=all_rows):
        return feats.at[c, k, q, part_rows]

    def across(k, q, name):
        send(block(k, q), block(k, q), me, name, k, core=1 - c)

    def sides(k):
        for to, name, tname in ((ex, "xr", "tx"), (ey, "yr", "ty")):
            send(shares.at[k, j], shares.at[k, j], to, tname, k)
            send(block(k, j), block(k, j), to, name, k)

    def column(k):
        landed(shares.at[k, j], "tz", k)
        landed(block(k, j), "zr", k)
        to = jnp.where(k < z, me + PLANE, me - PLANE)
        send(shares.at[k, j], shares.at[k, j], to, "tz", k, when=inside)
        send(block(k, j), block(k, j), to, "zr", k, when=inside)
        across(k, j, "c0")

    def relay(k):
        landed(shares.at[k, yj], "ty", k)
        landed(shares.at[k, xj], "tx", k)
        send(shares.at[k, yj], shares.at[k, yj], ex, "td", k)
        landed(block(k, yj), "yr", k)
        send(block(k, yj, lo), block(k, yj, lo), ex, "dx", k)
        across(k, yj, "c2")
        landed(block(k, xj), "xr", k)
        send(block(k, xj, hi), block(k, xj, hi), ey, "dy", k)
        across(k, xj, "c1")

    def corner(k):
        landed(shares.at[k, dj], "td", k)
        landed(block(k, dj, lo), "dx", k)
        landed(block(k, dj, hi), "dy", k)
        across(k, dj, "c3")

    def other_core(k):
        for q, name in ((j, "c0"), (xj, "c1"), (yj, "c2"), (dj, "c3")):
            landed(feats.at[1 - c, k, q], name, k)

    def my_share(k):
        lanes = shares.shape[-1]
        row, off = me * rows // lanes, me * rows % lanes
        lane = lax.broadcasted_iota(jnp.int32, (rows, lanes), 1)
        line = lax.broadcasted_iota(jnp.int32, (rows, lanes), 0)
        columns = []
        for q in range(PLANE):
            values = jnp.broadcast_to(shares[k, q, pl.ds(row, 1), :], (rows, lanes))
            columns.append(jnp.sum(jnp.where(lane == line + off, values, 0.0), axis=1, keepdims=True))
        return jnp.concatenate(columns, axis=0)

    def up_side(k, w):
        total = None
        for side in range(2):
            x = feats[side, k].reshape(PLANE * rows, width)
            wg = w_gate[:, :, side * width:(side + 1) * width].reshape(2 * units, width)
            term = lax.dot_general(x, wg, (((1,), (1,)), ((), ())), preferred_element_type=jnp.float32)
            total = term if total is None else total + term
        gate, upward = total[:, :units], total[:, units:]
        value = gate / (1.0 + jnp.exp(-gate)) * upward
        hid[c, k] = jnp.where(w > 0, value, 0.0).astype(jnp.bfloat16)
        send(hid.at[c, k], hid.at[c, k], me, "hr", k, core=1 - c)

    def down_side(k, w, first):
        landed(hid.at[1 - c, k], "hr", k)
        mine = hid[c, k]
        for side in range(2):
            cols = slice(side * units, (side + 1) * units)
            gram = lax.dot_general(mine, hid[side, k], (((0,), (0,)), ((), ())),
                                   preferred_element_type=jnp.float32)
            hess[0, :, cols] = gram if first else hess[0, :, cols] + gram
        step = 512
        for start in range(0, width, step):
            cols = slice(start, start + step)
            o = jnp.dot(hid[0, k], w_down[:units, cols], preferred_element_type=jnp.float32)
            o = o + jnp.dot(hid[1, k], w_down[units:, cols], preferred_element_type=jnp.float32)
            part[k, :, :, cols] = (o * w).astype(jnp.bfloat16).reshape(PLANE, rows, step)

    def give(k):
        send(part.at[k, dj, lo], got_ax.at[k], ex, "ax", k)
        send(part.at[k, dj, hi], got_ay.at[k], ey, "ay", k)
        send(part.at[k, xj, lo], got_bx.at[k, lo], ex, "bx0", k)
        send(part.at[k, yj, hi], got_by.at[k, hi], ey, "by1", k)

    def add_up(*terms):
        total = terms[0].astype(jnp.float32)
        for term in terms[1:]:
            total = total + term.astype(jnp.float32)
        return total.astype(jnp.bfloat16)

    def pass_on(k):
        landed(got_ax.at[k], "ax", k)
        part[k, yj, lo] = add_up(part[k, yj, lo], got_ax[k])
        send(part.at[k, yj, lo], got_by.at[k, lo], ey, "by0", k)
        landed(got_ay.at[k], "ay", k)
        part[k, xj, hi] = add_up(part[k, xj, hi], got_ay[k])
        send(part.at[k, xj, hi], got_bx.at[k, hi], ex, "bx1", k)

    def plane_done(k):
        landed(got_bx.at[k, lo], "bx0", k)
        landed(got_bx.at[k, hi], "bx1", k)
        landed(got_by.at[k, lo], "by0", k)
        landed(got_by.at[k, hi], "by1", k)

    def z_sem(slot, k):
        return recv_sem.at[(NAMES.index("z0") + slot) * PLANES + k]

    def z_copy(k):
        slot = jnp.where(k > z, 0, 1)
        to = jnp.where(k > z, me + PLANE, me - PLANE)
        copy = pltpu.make_async_remote_copy(
            src_ref=part.at[k, j], dst_ref=got_z.at[slot, k], send_sem=send_sem.at[len(started)],
            recv_sem=z_sem(slot, k), device_id=(to, c), device_id_type=pl.DeviceIdType.MESH)
        return copy, slot

    def chain_end(k):
        copy, _ = z_copy(k)
        started.append((copy, at_end))

        @pl.when(at_end)
        def _():
            plane_done(k)
            part[k, j] = add_up(part[k, j], got_bx[k], got_by[k])
            copy.start()

    def chain_inside(k):
        copy, slot = z_copy(k)
        started.append((copy, inside))

        @pl.when(inside)
        def _():
            plane_done(k)
            copy.wait_recv()
            part[k, j] = add_up(part[k, j], got_bx[k], got_by[k], got_z[slot, k])
            copy.start()

    feats[c, z, j] = tokens[...]
    shares[z, j] = table[...]
    barrier = pltpu.get_barrier_semaphore()

    def greet(to, core):
        pl.semaphore_signal(barrier, inc=1, device_id=(to, core), device_id_type=pl.DeviceIdType.MESH)

    greet(me, 1 - c)
    greet(ex, c)
    greet(ey, c)
    pl.when(z > 0)(lambda: greet(me - PLANE, c))
    pl.when(z < PLANES - 1)(lambda: greet(me + PLANE, c))
    pl.when(at_end)(lambda: pl.semaphore_wait(barrier, 4))
    pl.when(inside)(lambda: pl.semaphore_wait(barrier, 5))

    for to, when in ((me - PLANE, z > 0), (me + PLANE, z < PLANES - 1)):
        send(shares.at[z, j], shares.at[z, j], to, "tz", z, when=when)
        send(block(z, j), block(z, j), to, "zr", z, when=when)
    sides(z)
    across(z, j, "c0")
    column(a1)
    sides(a1)
    relay(order[0])
    column(a2)
    corner(order[0])
    relay(order[1])
    column(a3)
    sides(a3)
    sides(a2)

    load_gate.wait()
    load_down.wait()
    count = None
    for i, k in enumerate(order):
        other_core(k)
        w = my_share(k)
        hits = jnp.sum((w > 0).astype(jnp.float32), axis=0, keepdims=True)
        count = hits if count is None else count + hits
        up_side(k, w)
        if i + 2 < PLANES:
            relay(order[i + 2])
        down_side(k, w, i == 0)
        give(k)
        if i + 1 < PLANES:
            corner(order[i + 1])
        if i >= 1:
            pass_on(order[i - 1])
        if i >= 2:
            chain_end(order[i - 1])
    pass_on(order[3])
    hess[0] = hess[0] * (2.0 / count)
    chain_end(order[3])
    chain_inside(a3)
    chain_inside(pick((0, 0, 3, 0), z))
    chain_inside(pick((0, 2, 1, 0), z))
    plane_done(z)

    @pl.when(at_end)
    def _():
        slot = jnp.where(z > 0, 0, 1)
        pltpu.make_async_remote_copy(
            src_ref=part.at[z, j], dst_ref=got_z.at[slot, z], send_sem=send_sem.at[0],
            recv_sem=z_sem(slot, z), device_id=(me, 1 - c),
            device_id_type=pl.DeviceIdType.MESH).wait_recv()
        out[...] = add_up(part[z, j], got_bx[z], got_by[z], got_z[slot, z])

    @pl.when(inside)
    def _():
        landed(got_z.at[0, z], "z0", z)
        landed(got_z.at[1, z], "z1", z)
        out[...] = add_up(part[z, j], got_bx[z], got_by[z], got_z[0, z], got_z[1, z])

    for copy, when in started:
        if when is None:
            copy.wait_send()
        else:
            pl.when(when)(copy.wait_send)


def kernel_body(tokens, route_ids, route_weights, gate_up, down_proj):
    rows, width = tokens.shape
    experts = lax.axis_size("expert")
    units = gate_up.shape[2]
    lanes = 128
    share = route_weights / jnp.sum(route_weights, axis=1, keepdims=True)
    hit = route_ids[None] == jnp.arange(experts, dtype=jnp.int32)[:, None, None]
    table = jnp.sum(jnp.where(hit, share[None], 0.0), axis=2).reshape(experts * rows // lanes, lanes)
    bf, f32 = jnp.bfloat16, jnp.float32
    out, hess = pl.pallas_call(
        layer_kernel,
        out_shape=(
            jax.ShapeDtypeStruct((rows, width), bf),
            jax.ShapeDtypeStruct((1, units, 2 * units), f32),
        ),
        in_specs=[pl.BlockSpec(memory_space=pltpu.VMEM)] * 2 + [pl.BlockSpec(memory_space=pl.ANY)] * 2,
        out_specs=(pl.BlockSpec(memory_space=pltpu.VMEM),) * 2,
        scratch_shapes=[
            pltpu.VMEM((2, PLANES, PLANE, rows, width), bf),
            pltpu.VMEM((PLANES, PLANE) + table.shape, f32),
            pltpu.VMEM((2, PLANES, PLANE * rows, units), bf),
            pltpu.VMEM((PLANES, PLANE, rows, width), bf),
            pltpu.VMEM((PLANES, rows // 2, width), bf),
            pltpu.VMEM((PLANES, rows // 2, width), bf),
            pltpu.VMEM((PLANES, rows, width), bf),
            pltpu.VMEM((PLANES, rows, width), bf),
            pltpu.VMEM((2, PLANES, rows, width), bf),
            pltpu.VMEM(gate_up.shape[1:], bf),
            pltpu.VMEM(down_proj.shape[1:], bf),
            pltpu.SemaphoreType.DMA((SENDS,)),
            pltpu.SemaphoreType.DMA((len(NAMES) * PLANES,)),
            pltpu.SemaphoreType.DMA((2,)),
        ],
        compiler_params=pltpu.CompilerParams(
            collective_id=0, has_side_effects=True, vmem_limit_bytes=56 * 1024 * 1024
        ),
        name="moe_layer",
    )(tokens, table, gate_up, down_proj)
    return (out, hess)


def body(tokens, route_ids, route_weights, gate_up, down_proj):
    local_experts = gate_up.shape[0]
    all_experts = local_experts * lax.axis_size("expert")
    share = route_weights / jnp.sum(route_weights, axis=1, keepdims=True)
    hit = route_ids[:, :, None] == jnp.arange(all_experts, dtype=jnp.int32)[None, None, :]
    table = jnp.sum(jnp.where(hit, share[:, :, None], 0.0), axis=1)
    table = lax.all_gather(table.T, "expert", axis=1, tiled=True)
    mine = lax.dynamic_slice_in_dim(
        table, lax.axis_index("expert") * local_experts, local_experts, axis=0
    )
    features = lax.all_gather(tokens, "expert", axis=0, tiled=True)
    features = lax.all_gather(features, "hidden", axis=1, tiled=True)
    routed = jnp.sum((mine > 0).astype(jnp.float32), axis=1)
    gate = jnp.einsum("td,efd->etf", features, gate_up[:, 0], preferred_element_type=jnp.float32)
    upward = jnp.einsum("td,efd->etf", features, gate_up[:, 1], preferred_element_type=jnp.float32)
    hidden = jnp.where((mine > 0)[:, :, None], jax.nn.silu(gate) * upward, 0.0).astype(jnp.bfloat16)
    rows = lax.all_gather(hidden, "hidden", axis=2, tiled=True)
    columns = jnp.einsum("etf,etg->efg", hidden, rows, preferred_element_type=jnp.float32)
    hessian = columns * (2.0 / routed)[:, None, None]
    out = jnp.einsum("etg,egd->etd", rows, down_proj, preferred_element_type=jnp.float32)
    out = jnp.sum(out * mine[:, :, None], axis=0).astype(jnp.bfloat16)
    layer_out = lax.psum_scatter(out, "expert", scatter_dimension=0, tiled=True)
    return (layer_out, hessian)


def solution(mesh):
    in_plane = mesh.shape["expert"] == PLANES * PLANE and mesh.shape["hidden"] == 2
    return jax.shard_map(
        kernel_body if in_plane else body,
        mesh=mesh,
        in_specs=(
            P("expert", "hidden"),
            P("expert", None),
            P("expert", None),
            P("expert", None, "hidden", None),
            P("expert", None, "hidden"),
        ),
        out_specs=(P("expert", "hidden"), P("expert", "hidden", None)),
        check_vma=False,
    )
```

```python
import jax
import jax.numpy as jnp
from jax import lax
from jax.experimental import pallas as pl
from jax.experimental.pallas import tpu as pltpu
from jax.sharding import PartitionSpec as P

PLANES = 4
PLANE = 4
FIRST = (1, 2, 1, 2)
SECOND = (2, 0, 3, 1)
THIRD = (3, 3, 0, 0)
NAMES = ("zr", "xr", "yr", "dx", "dy", "c0", "c1", "c2", "c3", "tz", "tx", "ty", "td", "hr",
         "ax", "ay", "bx0", "bx1", "by0", "by1", "z00", "z01", "z10", "z11")
SENDS = 128


def pick(values, z):
    chosen = jnp.int32(values[0])
    for place in range(1, len(values)):
        chosen = jnp.where(z == place, jnp.int32(values[place]), chosen)
    return chosen


def layer_kernel(tokens, ids, weights, gate_up, down, out, hess,
                 feats, shares, hid, part, got_ax, got_ay, got_bx, got_by, got_z,
                 w_gate, w_down, send_sem, recv_sem, load_sem):
    rows, width = tokens.shape
    half = rows // 2
    units = hid.shape[-1]
    me = lax.axis_index("expert")
    c = lax.axis_index("hidden")
    z, j = me // PLANE, me % PLANE
    xj, yj, dj = j + 1 - 2 * (j % 2), (j + 2) % PLANE, PLANE - 1 - j
    ex, ey = z * PLANE + xj, z * PLANE + yj
    at_end = z % (PLANES - 1) == 0
    inside = z % (PLANES - 1) != 0
    a1, a2, a3 = pick(FIRST, z), pick(SECOND, z), pick(THIRD, z)
    lo, hi = pl.ds(0, half), pl.ds(half, half)
    all_rows = pl.ds(0, rows)
    started = []

    load_gate = pltpu.make_async_copy(gate_up.at[0], w_gate, load_sem.at[0])
    load_down = pltpu.make_async_copy(down.at[0], w_down, load_sem.at[1])
    load_gate.start()
    load_down.start()

    def sem(name, k):
        return recv_sem.at[NAMES.index(name) * PLANES + k]

    def send(src, dst, to, name, k, core=None, when=None):
        copy = pltpu.make_async_remote_copy(
            src_ref=src, dst_ref=dst, send_sem=send_sem.at[len(started)], recv_sem=sem(name, k),
            device_id=(to, c if core is None else core), device_id_type=pl.DeviceIdType.MESH)
        started.append((copy, when))
        if when is None:
            copy.start()
        else:
            pl.when(when)(copy.start)

    def landed(dst, name, k):
        pltpu.make_async_remote_copy(
            src_ref=dst, dst_ref=dst, send_sem=send_sem.at[0], recv_sem=sem(name, k),
            device_id=(me, 1 - c), device_id_type=pl.DeviceIdType.MESH).wait_recv()

    def block(k, q, part_rows=all_rows):
        return feats.at[c, k, q, part_rows]

    def across(k, q, name):
        send(block(k, q), block(k, q), me, name, k, core=1 - c)

    def sides(k):
        for to, name, tname in ((ex, "xr", "tx"), (ey, "yr", "ty")):
            send(shares.at[k, j], shares.at[k, j], to, tname, k)
            send(block(k, j), block(k, j), to, name, k)

    def column(k):
        landed(shares.at[k, j], "tz", k)
        landed(block(k, j), "zr", k)
        to = jnp.where(k < z, me + PLANE, me - PLANE)
        send(shares.at[k, j], shares.at[k, j], to, "tz", k, when=inside)
        send(block(k, j), block(k, j), to, "zr", k, when=inside)
        across(k, j, "c0")

    def relay(k):
        landed(shares.at[k, yj], "ty", k)
        landed(shares.at[k, xj], "tx", k)
        send(shares.at[k, yj], shares.at[k, yj], ex, "td", k)
        landed(block(k, yj), "yr", k)
        send(block(k, yj, lo), block(k, yj, lo), ex, "dx", k)
        across(k, yj, "c2")
        landed(block(k, xj), "xr", k)
        send(block(k, xj, hi), block(k, xj, hi), ey, "dy", k)
        across(k, xj, "c1")

    def corner(k):
        landed(shares.at[k, dj], "td", k)
        landed(block(k, dj, lo), "dx", k)
        landed(block(k, dj, hi), "dy", k)
        across(k, dj, "c3")

    def other_core(k):
        for q, name in ((j, "c0"), (xj, "c1"), (yj, "c2"), (dj, "c3")):
            landed(feats.at[1 - c, k, q], name, k)

    def share_table():
        lanes = shares.shape[-1]
        share = weights[...] / jnp.sum(weights[...], axis=1, keepdims=True)
        lane = lax.broadcasted_iota(jnp.int32, (rows, lanes), 1)
        dense = jnp.zeros((rows, lanes), jnp.float32)
        for q in range(ids.shape[1]):
            dense = dense + jnp.where(ids[:, q:q + 1] == lane, share[:, q:q + 1], 0.0)
        square = jnp.concatenate([dense, jnp.zeros((lanes - rows, lanes), jnp.float32)], axis=0)
        shares[z, j] = square.T[:shares.shape[2]]

    def my_share(k):
        lanes = shares.shape[-1]
        lane = lax.broadcasted_iota(jnp.int32, (rows, lanes), 1)
        line = lax.broadcasted_iota(jnp.int32, (rows, lanes), 0)
        columns = []
        for q in range(PLANE):
            values = jnp.broadcast_to(shares[k, q, pl.ds(me, 1), :], (rows, lanes))
            columns.append(jnp.sum(jnp.where(lane == line, values, 0.0), axis=1, keepdims=True))
        return jnp.concatenate(columns, axis=0)

    def up_side(k, w):
        total = None
        for side in range(2):
            x = feats[side, k].reshape(PLANE * rows, width)
            wg = w_gate[:, :, side * width:(side + 1) * width].reshape(2 * units, width)
            term = lax.dot_general(x, wg, (((1,), (1,)), ((), ())), preferred_element_type=jnp.float32)
            total = term if total is None else total + term
        gate, upward = total[:, :units], total[:, units:]
        value = gate / (1.0 + jnp.exp(-gate)) * upward
        hid[c, k] = jnp.where(w > 0, value, 0.0).astype(jnp.bfloat16)
        send(hid.at[c, k], hid.at[c, k], me, "hr", k, core=1 - c)

    def down_side(k, w, first):
        landed(hid.at[1 - c, k], "hr", k)
        mine = hid[c, k]
        for side in range(2):
            cols = slice(side * units, (side + 1) * units)
            gram = lax.dot_general(mine, hid[side, k], (((0,), (0,)), ((), ())),
                                   preferred_element_type=jnp.float32)
            hess[0, :, cols] = gram if first else hess[0, :, cols] + gram
        step = 512
        for start in range(0, width, step):
            cols = slice(start, start + step)
            o = jnp.dot(hid[0, k], w_down[:units, cols], preferred_element_type=jnp.float32)
            o = o + jnp.dot(hid[1, k], w_down[units:, cols], preferred_element_type=jnp.float32)
            part[k, :, :, cols] = (o * w).astype(jnp.bfloat16).reshape(PLANE, rows, step)

    def give(k):
        send(part.at[k, dj, lo], got_ax.at[k], ex, "ax", k)
        send(part.at[k, dj, hi], got_ay.at[k], ey, "ay", k)
        send(part.at[k, xj, lo], got_bx.at[k, lo], ex, "bx0", k)
        send(part.at[k, yj, hi], got_by.at[k, hi], ey, "by1", k)

    def add_up(*terms):
        total = terms[0].astype(jnp.float32)
        for term in terms[1:]:
            total = total + term.astype(jnp.float32)
        return total.astype(jnp.bfloat16)

    def pass_on(k):
        landed(got_ax.at[k], "ax", k)
        part[k, yj, lo] = add_up(part[k, yj, lo], got_ax[k])
        send(part.at[k, yj, lo], got_by.at[k, lo], ey, "by0", k)
        landed(got_ay.at[k], "ay", k)
        part[k, xj, hi] = add_up(part[k, xj, hi], got_ay[k])
        send(part.at[k, xj, hi], got_bx.at[k, hi], ex, "bx1", k)

    def plane_done(k):
        landed(got_bx.at[k, lo], "bx0", k)
        landed(got_bx.at[k, hi], "bx1", k)
        landed(got_by.at[k, lo], "by0", k)
        landed(got_by.at[k, hi], "by1", k)

    pieces = [slice(0, width // 2), slice(width // 2, width)]

    def z_sem(slot, k, p):
        return recv_sem.at[(NAMES.index("z00") + 2 * slot + p) * PLANES + k]

    def z_copies(k, when):
        slot = jnp.where(k > z, 0, 1)
        to = jnp.where(k > z, me + PLANE, me - PLANE)
        copies = []
        for p, cols in enumerate(pieces):
            copy = pltpu.make_async_remote_copy(
                src_ref=part.at[k, j, :, cols], dst_ref=got_z.at[slot, k, :, cols],
                send_sem=send_sem.at[len(started)], recv_sem=z_sem(slot, k, p),
                device_id=(to, c), device_id_type=pl.DeviceIdType.MESH)
            started.append((copy, when))
            copies.append(copy)
        return copies, slot

    def z_landed(slot, k, p):
        dst = got_z.at[slot, k, :, pieces[p]]
        pltpu.make_async_remote_copy(
            src_ref=dst, dst_ref=dst, send_sem=send_sem.at[0], recv_sem=z_sem(slot, k, p),
            device_id=(me, 1 - c), device_id_type=pl.DeviceIdType.MESH).wait_recv()

    def chain_end(k):
        copies, _ = z_copies(k, at_end)

        @pl.when(at_end)
        def _():
            plane_done(k)
            for copy, cols in zip(copies, pieces):
                part[k, j, :, cols] = add_up(part[k, j, :, cols], got_bx[k, :, cols], got_by[k, :, cols])
                copy.start()

    def chain_inside(k):
        copies, slot = z_copies(k, inside)

        @pl.when(inside)
        def _():
            plane_done(k)
            for p, cols in enumerate(pieces):
                z_landed(slot, k, p)
                part[k, j, :, cols] = add_up(part[k, j, :, cols], got_bx[k, :, cols], got_by[k, :, cols],
                                             got_z[slot, k, :, cols])
                copies[p].start()

    feats[c, z, j] = tokens[...]
    barrier = pltpu.get_barrier_semaphore()

    def greet(to, core):
        pl.semaphore_signal(barrier, inc=1, device_id=(to, core), device_id_type=pl.DeviceIdType.MESH)

    greet(me, 1 - c)
    greet(ex, c)
    greet(ey, c)
    pl.when(z > 0)(lambda: greet(me - PLANE, c))
    pl.when(z < PLANES - 1)(lambda: greet(me + PLANE, c))
    pl.when(at_end)(lambda: pl.semaphore_wait(barrier, 4))
    pl.when(inside)(lambda: pl.semaphore_wait(barrier, 5))

    for to, when in ((me - PLANE, z > 0), (me + PLANE, z < PLANES - 1)):
        send(block(z, j), block(z, j), to, "zr", z, when=when)
    send(block(z, j), block(z, j), ex, "xr", z)
    send(block(z, j), block(z, j), ey, "yr", z)
    across(z, j, "c0")
    share_table()
    for to, when in ((me - PLANE, z > 0), (me + PLANE, z < PLANES - 1)):
        send(shares.at[z, j], shares.at[z, j], to, "tz", z, when=when)
    send(shares.at[z, j], shares.at[z, j], ex, "tx", z)
    send(shares.at[z, j], shares.at[z, j], ey, "ty", z)
    column(a1)
    sides(a1)
    relay(z)
    column(a2)
    corner(z)
    relay(a1)
    column(a3)
    sides(a3)
    sides(a2)

    load_gate.wait()
    load_down.wait()

    def up_round(k):
        other_core(k)
        w = my_share(k)
        up_side(k, w)
        return w, jnp.sum((w > 0).astype(jnp.float32), axis=0, keepdims=True)

    w, count = up_round(z)
    corner(a1)
    down_side(z, w, True)
    relay(a3)

    w, hits = up_round(a1)
    count = count + hits
    relay(a2)
    down_side(a1, w, False)
    give(a1)
    corner(a3)

    w, hits = up_round(a3)
    count = count + hits
    corner(a2)
    down_side(a3, w, False)
    give(a3)
    pass_on(a1)

    w, hits = up_round(a2)
    count = count + hits
    down_side(a2, w, False)
    give(a2)

    pass_on(a3)
    chain_end(a1)
    pass_on(a2)
    give(z)
    hess[0] = hess[0] * (2.0 / count)
    chain_end(a3)
    chain_inside(a3)
    pass_on(z)
    chain_end(a2)
    chain_inside(pick((0, 0, 3, 0), z))
    chain_inside(pick((0, 2, 1, 0), z))
    plane_done(z)

    @pl.when(at_end)
    def _():
        slot = jnp.where(z > 0, 0, 1)
        for p, cols in enumerate(pieces):
            z_landed(slot, z, p)
            out[:, cols] = add_up(part[z, j, :, cols], got_bx[z, :, cols], got_by[z, :, cols],
                                  got_z[slot, z, :, cols])

    @pl.when(inside)
    def _():
        for p, cols in enumerate(pieces):
            z_landed(0, z, p)
            z_landed(1, z, p)
            out[:, cols] = add_up(part[z, j, :, cols], got_bx[z, :, cols], got_by[z, :, cols],
                                  got_z[0, z, :, cols], got_z[1, z, :, cols])

    for copy, when in started:
        if when is None:
            copy.wait_send()
        else:
            pl.when(when)(copy.wait_send)


def kernel_body(tokens, route_ids, route_weights, gate_up, down_proj):
    rows, width = tokens.shape
    experts = lax.axis_size("expert")
    units = gate_up.shape[2]
    lanes = 128
    bf, f32 = jnp.bfloat16, jnp.float32
    out, hess = pl.pallas_call(
        layer_kernel,
        out_shape=(
            jax.ShapeDtypeStruct((rows, width), bf),
            jax.ShapeDtypeStruct((1, units, 2 * units), f32),
        ),
        in_specs=[pl.BlockSpec(memory_space=pltpu.VMEM)] * 3 + [pl.BlockSpec(memory_space=pl.ANY)] * 2,
        out_specs=(pl.BlockSpec(memory_space=pltpu.VMEM),) * 2,
        scratch_shapes=[
            pltpu.VMEM((2, PLANES, PLANE, rows, width), bf),
            pltpu.VMEM((PLANES, PLANE, experts, lanes), f32),
            pltpu.VMEM((2, PLANES, PLANE * rows, units), bf),
            pltpu.VMEM((PLANES, PLANE, rows, width), bf),
            pltpu.VMEM((PLANES, rows // 2, width), bf),
            pltpu.VMEM((PLANES, rows // 2, width), bf),
            pltpu.VMEM((PLANES, rows, width), bf),
            pltpu.VMEM((PLANES, rows, width), bf),
            pltpu.VMEM((2, PLANES, rows, width), bf),
            pltpu.VMEM(gate_up.shape[1:], bf),
            pltpu.VMEM(down_proj.shape[1:], bf),
            pltpu.SemaphoreType.DMA((SENDS,)),
            pltpu.SemaphoreType.DMA((len(NAMES) * PLANES,)),
            pltpu.SemaphoreType.DMA((2,)),
        ],
        compiler_params=pltpu.CompilerParams(
            collective_id=0, has_side_effects=True, vmem_limit_bytes=56 * 1024 * 1024
        ),
        name="moe_layer",
    )(tokens, route_ids, route_weights, gate_up, down_proj)
    return (out, hess)


def body(tokens, route_ids, route_weights, gate_up, down_proj):
    local_experts = gate_up.shape[0]
    all_experts = local_experts * lax.axis_size("expert")
    share = route_weights / jnp.sum(route_weights, axis=1, keepdims=True)
    hit = route_ids[:, :, None] == jnp.arange(all_experts, dtype=jnp.int32)[None, None, :]
    table = jnp.sum(jnp.where(hit, share[:, :, None], 0.0), axis=1)
    table = lax.all_gather(table.T, "expert", axis=1, tiled=True)
    mine = lax.dynamic_slice_in_dim(
        table, lax.axis_index("expert") * local_experts, local_experts, axis=0
    )
    features = lax.all_gather(tokens, "expert", axis=0, tiled=True)
    features = lax.all_gather(features, "hidden", axis=1, tiled=True)
    routed = jnp.sum((mine > 0).astype(jnp.float32), axis=1)
    gate = jnp.einsum("td,efd->etf", features, gate_up[:, 0], preferred_element_type=jnp.float32)
    upward = jnp.einsum("td,efd->etf", features, gate_up[:, 1], preferred_element_type=jnp.float32)
    hidden = jnp.where((mine > 0)[:, :, None], jax.nn.silu(gate) * upward, 0.0).astype(jnp.bfloat16)
    rows = lax.all_gather(hidden, "hidden", axis=2, tiled=True)
    columns = jnp.einsum("etf,etg->efg", hidden, rows, preferred_element_type=jnp.float32)
    hessian = columns * (2.0 / routed)[:, None, None]
    out = jnp.einsum("etg,egd->etd", rows, down_proj, preferred_element_type=jnp.float32)
    out = jnp.sum(out * mine[:, :, None], axis=0).astype(jnp.bfloat16)
    layer_out = lax.psum_scatter(out, "expert", scatter_dimension=0, tiled=True)
    return (layer_out, hessian)


def solution(mesh):
    in_plane = mesh.shape["expert"] == PLANES * PLANE and mesh.shape["hidden"] == 2
    return jax.shard_map(
        kernel_body if in_plane else body,
        mesh=mesh,
        in_specs=(
            P("expert", "hidden"),
            P("expert", None),
            P("expert", None),
            P("expert", None, "hidden", None),
            P("expert", None, "hidden"),
        ),
        out_specs=(P("expert", "hidden"), P("expert", "hidden", None)),
        check_vma=False,
    )
```

```python
import jax
import jax.numpy as jnp
from jax import lax
from jax.experimental import pallas as pl
from jax.experimental.pallas import tpu as pltpu
from jax.sharding import PartitionSpec as P

PLANES = 4
PLANE = 4
FIRST = (1, 2, 1, 2)
SECOND = (2, 0, 3, 1)
THIRD = (3, 3, 0, 0)
NAMES = ("zr", "xr", "yr", "dx", "dy", "c0", "c1", "c2", "c3", "tz", "tx", "ty", "td", "hr",
         "ax", "ay", "bx0", "bx1", "by0", "by1", "z00", "z01", "z10", "z11")
SENDS = 128


def pick(values, z):
    chosen = jnp.int32(values[0])
    for place in range(1, len(values)):
        chosen = jnp.where(z == place, jnp.int32(values[place]), chosen)
    return chosen


def layer_kernel(tokens, ids, weights, gate_up, down, out, hess_out,
                 feats, shares, hid, part, got_ax, got_ay, got_bx, got_by, got_z,
                 w_gate, w_down, hess, send_sem, recv_sem, load_sem):
    rows, width = tokens.shape
    half = rows // 2
    units = hid.shape[-1]
    me = lax.axis_index("expert")
    c = lax.axis_index("hidden")
    z, j = me // PLANE, me % PLANE
    xj, yj, dj = j + 1 - 2 * (j % 2), (j + 2) % PLANE, PLANE - 1 - j
    ex, ey = z * PLANE + xj, z * PLANE + yj
    at_end = z % (PLANES - 1) == 0
    inside = z % (PLANES - 1) != 0
    a1, a2, a3 = pick(FIRST, z), pick(SECOND, z), pick(THIRD, z)
    lo, hi = pl.ds(0, half), pl.ds(half, half)
    all_rows = pl.ds(0, rows)
    started = []

    load_gate = pltpu.make_async_copy(gate_up.at[0], w_gate, load_sem.at[0])
    load_down = pltpu.make_async_copy(down.at[0], w_down, load_sem.at[1])
    load_gate.start()
    load_down.start()

    def sem(name, k):
        return recv_sem.at[NAMES.index(name) * PLANES + k]

    def send(src, dst, to, name, k, core=None, when=None):
        copy = pltpu.make_async_remote_copy(
            src_ref=src, dst_ref=dst, send_sem=send_sem.at[len(started)], recv_sem=sem(name, k),
            device_id=(to, c if core is None else core), device_id_type=pl.DeviceIdType.MESH)
        started.append((copy, when))
        if when is None:
            copy.start()
        else:
            pl.when(when)(copy.start)

    def landed(dst, name, k):
        pltpu.make_async_remote_copy(
            src_ref=dst, dst_ref=dst, send_sem=send_sem.at[0], recv_sem=sem(name, k),
            device_id=(me, 1 - c), device_id_type=pl.DeviceIdType.MESH).wait_recv()

    def block(k, q, part_rows=all_rows):
        return feats.at[c, k, q, part_rows]

    def across(k, q, name):
        send(block(k, q), block(k, q), me, name, k, core=1 - c)

    def sides(k):
        for to, name, tname in ((ex, "xr", "tx"), (ey, "yr", "ty")):
            send(shares.at[k, j], shares.at[k, j], to, tname, k)
            send(block(k, j), block(k, j), to, name, k)

    def column(k):
        landed(shares.at[k, j], "tz", k)
        landed(block(k, j), "zr", k)
        to = jnp.where(k < z, me + PLANE, me - PLANE)
        send(shares.at[k, j], shares.at[k, j], to, "tz", k, when=inside)
        send(block(k, j), block(k, j), to, "zr", k, when=inside)
        across(k, j, "c0")

    def relay(k):
        landed(shares.at[k, yj], "ty", k)
        landed(shares.at[k, xj], "tx", k)
        send(shares.at[k, yj], shares.at[k, yj], ex, "td", k)
        landed(block(k, yj), "yr", k)
        send(block(k, yj, lo), block(k, yj, lo), ex, "dx", k)
        across(k, yj, "c2")
        landed(block(k, xj), "xr", k)
        send(block(k, xj, hi), block(k, xj, hi), ey, "dy", k)
        across(k, xj, "c1")

    def corner(k):
        landed(shares.at[k, dj], "td", k)
        landed(block(k, dj, lo), "dx", k)
        landed(block(k, dj, hi), "dy", k)
        across(k, dj, "c3")

    def other_core(k):
        for q, name in ((j, "c0"), (xj, "c1"), (yj, "c2"), (dj, "c3")):
            landed(feats.at[1 - c, k, q], name, k)

    def share_table():
        experts, lanes = shares.shape[2:]
        share = weights[...] / jnp.sum(weights[...], axis=0, keepdims=True)
        expert = lax.broadcasted_iota(jnp.int32, (experts, rows), 0)
        dense = jnp.zeros((experts, rows), jnp.float32)
        for q in range(ids.shape[0]):
            dense = dense + jnp.where(ids[q:q + 1, :] == expert, share[q:q + 1, :], 0.0)
        shares[z, j] = jnp.concatenate([dense, jnp.zeros((experts, lanes - rows), jnp.float32)], axis=1)

    def my_share(k):
        lanes = shares.shape[-1]
        lane = lax.broadcasted_iota(jnp.int32, (rows, lanes), 1)
        line = lax.broadcasted_iota(jnp.int32, (rows, lanes), 0)
        columns = []
        for q in range(PLANE):
            values = jnp.broadcast_to(shares[k, q, pl.ds(me, 1), :], (rows, lanes))
            columns.append(jnp.sum(jnp.where(lane == line, values, 0.0), axis=1, keepdims=True))
        return jnp.concatenate(columns, axis=0)

    def up_side(k, w):
        total = None
        for side in range(2):
            x = feats[side, k].reshape(PLANE * rows, width)
            wg = w_gate[:, :, side * width:(side + 1) * width].reshape(2 * units, width)
            term = lax.dot_general(x, wg, (((1,), (1,)), ((), ())), preferred_element_type=jnp.float32)
            total = term if total is None else total + term
        gate, upward = total[:, :units], total[:, units:]
        value = gate / (1.0 + jnp.exp(-gate)) * upward
        hid[c, k] = jnp.where(w > 0, value, 0.0).astype(jnp.bfloat16)
        send(hid.at[c, k], hid.at[c, k], me, "hr", k, core=1 - c)

    def down_side(k, w, first):
        landed(hid.at[1 - c, k], "hr", k)
        mine = hid[c, k]
        for side in range(2):
            cols = slice(side * units, (side + 1) * units)
            gram = lax.dot_general(mine, hid[side, k], (((0,), (0,)), ((), ())),
                                   preferred_element_type=jnp.float32)
            hess[:, cols] = gram if first else hess[:, cols] + gram
        step = 512
        for start in range(0, width, step):
            cols = slice(start, start + step)
            o = jnp.dot(hid[0, k], w_down[:units, cols], preferred_element_type=jnp.float32)
            o = o + jnp.dot(hid[1, k], w_down[units:, cols], preferred_element_type=jnp.float32)
            part[k, :, :, cols] = (o * w).astype(jnp.bfloat16).reshape(PLANE, rows, step)

    def give(k):
        send(part.at[k, dj, lo], got_ax.at[k], ex, "ax", k)
        send(part.at[k, dj, hi], got_ay.at[k], ey, "ay", k)
        send(part.at[k, xj, lo], got_bx.at[k, lo], ex, "bx0", k)
        send(part.at[k, yj, hi], got_by.at[k, hi], ey, "by1", k)

    def add_up(*terms):
        total = terms[0].astype(jnp.float32)
        for term in terms[1:]:
            total = total + term.astype(jnp.float32)
        return total.astype(jnp.bfloat16)

    def pass_on(k):
        landed(got_ax.at[k], "ax", k)
        part[k, yj, lo] = add_up(part[k, yj, lo], got_ax[k])
        send(part.at[k, yj, lo], got_by.at[k, lo], ey, "by0", k)
        landed(got_ay.at[k], "ay", k)
        part[k, xj, hi] = add_up(part[k, xj, hi], got_ay[k])
        send(part.at[k, xj, hi], got_bx.at[k, hi], ex, "bx1", k)

    def plane_done(k):
        landed(got_bx.at[k, lo], "bx0", k)
        landed(got_bx.at[k, hi], "bx1", k)
        landed(got_by.at[k, lo], "by0", k)
        landed(got_by.at[k, hi], "by1", k)

    pieces = [slice(0, width // 2), slice(width // 2, width)]

    def z_sem(slot, k, p):
        return recv_sem.at[(NAMES.index("z00") + 2 * slot + p) * PLANES + k]

    def z_copies(k, when):
        slot = jnp.where(k > z, 0, 1)
        to = jnp.where(k > z, me + PLANE, me - PLANE)
        copies = []
        for p, cols in enumerate(pieces):
            copy = pltpu.make_async_remote_copy(
                src_ref=part.at[k, j, :, cols], dst_ref=got_z.at[slot, k, :, cols],
                send_sem=send_sem.at[len(started)], recv_sem=z_sem(slot, k, p),
                device_id=(to, c), device_id_type=pl.DeviceIdType.MESH)
            started.append((copy, when))
            copies.append(copy)
        return copies, slot

    def z_landed(slot, k, p):
        dst = got_z.at[slot, k, :, pieces[p]]
        pltpu.make_async_remote_copy(
            src_ref=dst, dst_ref=dst, send_sem=send_sem.at[0], recv_sem=z_sem(slot, k, p),
            device_id=(me, 1 - c), device_id_type=pl.DeviceIdType.MESH).wait_recv()

    def chain_end(k):
        copies, _ = z_copies(k, at_end)

        @pl.when(at_end)
        def _():
            plane_done(k)
            for copy, cols in zip(copies, pieces):
                part[k, j, :, cols] = add_up(part[k, j, :, cols], got_bx[k, :, cols], got_by[k, :, cols])
                copy.start()

    def chain_inside(k):
        copies, slot = z_copies(k, inside)

        @pl.when(inside)
        def _():
            plane_done(k)
            for p, cols in enumerate(pieces):
                z_landed(slot, k, p)
                part[k, j, :, cols] = add_up(part[k, j, :, cols], got_bx[k, :, cols], got_by[k, :, cols],
                                             got_z[slot, k, :, cols])
                copies[p].start()

    feats[c, z, j] = tokens[...]
    barrier = pltpu.get_barrier_semaphore()

    def greet(to, core):
        pl.semaphore_signal(barrier, inc=1, device_id=(to, core), device_id_type=pl.DeviceIdType.MESH)

    greet(me, 1 - c)
    greet(ex, c)
    greet(ey, c)
    pl.when(z > 0)(lambda: greet(me - PLANE, c))
    pl.when(z < PLANES - 1)(lambda: greet(me + PLANE, c))
    pl.when(at_end)(lambda: pl.semaphore_wait(barrier, 4))
    pl.when(inside)(lambda: pl.semaphore_wait(barrier, 5))

    for to, when in ((me - PLANE, z > 0), (me + PLANE, z < PLANES - 1)):
        send(block(z, j), block(z, j), to, "zr", z, when=when)
    send(block(z, j), block(z, j), ex, "xr", z)
    send(block(z, j), block(z, j), ey, "yr", z)
    across(z, j, "c0")
    share_table()
    for to, when in ((me - PLANE, z > 0), (me + PLANE, z < PLANES - 1)):
        send(shares.at[z, j], shares.at[z, j], to, "tz", z, when=when)
    send(shares.at[z, j], shares.at[z, j], ex, "tx", z)
    send(shares.at[z, j], shares.at[z, j], ey, "ty", z)
    column(a1)
    sides(a1)
    relay(z)
    column(a2)
    corner(z)
    relay(a1)
    column(a3)
    sides(a3)
    sides(a2)

    load_gate.wait()
    load_down.wait()

    def up_round(k):
        other_core(k)
        w = my_share(k)
        up_side(k, w)
        return w, jnp.sum((w > 0).astype(jnp.float32), axis=0, keepdims=True)

    w, count = up_round(z)
    corner(a1)
    down_side(z, w, True)
    relay(a3)

    w, hits = up_round(a1)
    count = count + hits
    relay(a2)
    down_side(a1, w, False)
    give(a1)
    corner(a3)

    w, hits = up_round(a3)
    count = count + hits
    corner(a2)
    down_side(a3, w, False)
    give(a3)
    pass_on(a1)

    w, hits = up_round(a2)
    count = count + hits
    down_side(a2, w, False)
    give(a2)

    pass_on(a3)
    chain_end(a1)
    pass_on(a2)
    give(z)
    hess[...] = hess[...] * (2.0 / count)
    store = pltpu.make_async_copy(hess, hess_out.at[0], load_sem.at[2])
    store.start()
    chain_end(a3)
    chain_inside(a3)
    pass_on(z)
    chain_end(a2)
    chain_inside(pick((0, 0, 3, 0), z))
    chain_inside(pick((0, 2, 1, 0), z))
    plane_done(z)

    @pl.when(at_end)
    def _():
        slot = jnp.where(z > 0, 0, 1)
        for p, cols in enumerate(pieces):
            z_landed(slot, z, p)
            out[:, cols] = add_up(part[z, j, :, cols], got_bx[z, :, cols], got_by[z, :, cols],
                                  got_z[slot, z, :, cols])

    @pl.when(inside)
    def _():
        for p, cols in enumerate(pieces):
            z_landed(0, z, p)
            z_landed(1, z, p)
            out[:, cols] = add_up(part[z, j, :, cols], got_bx[z, :, cols], got_by[z, :, cols],
                                  got_z[0, z, :, cols], got_z[1, z, :, cols])

    store.wait()
    for copy, when in started:
        if when is None:
            copy.wait_send()
        else:
            pl.when(when)(copy.wait_send)


def results_kernel(out_in, hess_in, out, hess, sem):
    copies = [pltpu.make_async_copy(out_in, out, sem.at[0]), pltpu.make_async_copy(hess_in, hess, sem.at[1])]
    for copy in copies:
        copy.start()
    for copy in copies:
        copy.wait()


def kernel_body(tokens, route_ids, route_weights, gate_up, down_proj):
    rows, width = tokens.shape
    experts = lax.axis_size("expert")
    units = gate_up.shape[2]
    lanes = 128
    bf, f32 = jnp.bfloat16, jnp.float32
    out, hess = pl.pallas_call(
        layer_kernel,
        out_shape=(
            jax.ShapeDtypeStruct((rows, width), bf),
            jax.ShapeDtypeStruct((1, units, 2 * units), f32),
        ),
        in_specs=[pl.BlockSpec(memory_space=pltpu.VMEM)] * 3 + [pl.BlockSpec(memory_space=pl.ANY)] * 2,
        out_specs=(pl.BlockSpec(memory_space=pltpu.VMEM), pl.BlockSpec(memory_space=pl.ANY)),
        scratch_shapes=[
            pltpu.VMEM((2, PLANES, PLANE, rows, width), bf),
            pltpu.VMEM((PLANES, PLANE, experts, lanes), f32),
            pltpu.VMEM((2, PLANES, PLANE * rows, units), bf),
            pltpu.VMEM((PLANES, PLANE, rows, width), bf),
            pltpu.VMEM((PLANES, rows // 2, width), bf),
            pltpu.VMEM((PLANES, rows // 2, width), bf),
            pltpu.VMEM((PLANES, rows, width), bf),
            pltpu.VMEM((PLANES, rows, width), bf),
            pltpu.VMEM((2, PLANES, rows, width), bf),
            pltpu.VMEM(gate_up.shape[1:], bf),
            pltpu.VMEM(down_proj.shape[1:], bf),
            pltpu.VMEM((units, 2 * units), f32),
            pltpu.SemaphoreType.DMA((SENDS,)),
            pltpu.SemaphoreType.DMA((len(NAMES) * PLANES,)),
            pltpu.SemaphoreType.DMA((3,)),
        ],
        compiler_params=pltpu.CompilerParams(
            collective_id=0, has_side_effects=True, vmem_limit_bytes=56 * 1024 * 1024
        ),
        name="moe_layer",
    )(tokens, route_ids.T, route_weights.T, gate_up, down_proj)
    return pl.pallas_call(
        results_kernel,
        out_shape=(jax.ShapeDtypeStruct(out.shape, out.dtype), jax.ShapeDtypeStruct(hess.shape, hess.dtype)),
        in_specs=[pl.BlockSpec(memory_space=pl.ANY)] * 2,
        out_specs=(pl.BlockSpec(memory_space=pl.ANY),) * 2,
        scratch_shapes=[pltpu.SemaphoreType.DMA((2,))],
        compiler_params=pltpu.CompilerParams(vmem_limit_bytes=56 * 1024 * 1024),
        name="results",
    )(out, hess)


def body(tokens, route_ids, route_weights, gate_up, down_proj):
    local_experts = gate_up.shape[0]
    all_experts = local_experts * lax.axis_size("expert")
    share = route_weights / jnp.sum(route_weights, axis=1, keepdims=True)
    hit = route_ids[:, :, None] == jnp.arange(all_experts, dtype=jnp.int32)[None, None, :]
    table = jnp.sum(jnp.where(hit, share[:, :, None], 0.0), axis=1)
    table = lax.all_gather(table.T, "expert", axis=1, tiled=True)
    mine = lax.dynamic_slice_in_dim(
        table, lax.axis_index("expert") * local_experts, local_experts, axis=0
    )
    features = lax.all_gather(tokens, "expert", axis=0, tiled=True)
    features = lax.all_gather(features, "hidden", axis=1, tiled=True)
    routed = jnp.sum((mine > 0).astype(jnp.float32), axis=1)
    gate = jnp.einsum("td,efd->etf", features, gate_up[:, 0], preferred_element_type=jnp.float32)
    upward = jnp.einsum("td,efd->etf", features, gate_up[:, 1], preferred_element_type=jnp.float32)
    hidden = jnp.where((mine > 0)[:, :, None], jax.nn.silu(gate) * upward, 0.0).astype(jnp.bfloat16)
    rows = lax.all_gather(hidden, "hidden", axis=2, tiled=True)
    columns = jnp.einsum("etf,etg->efg", hidden, rows, preferred_element_type=jnp.float32)
    hessian = columns * (2.0 / routed)[:, None, None]
    out = jnp.einsum("etg,egd->etd", rows, down_proj, preferred_element_type=jnp.float32)
    out = jnp.sum(out * mine[:, :, None], axis=0).astype(jnp.bfloat16)
    layer_out = lax.psum_scatter(out, "expert", scatter_dimension=0, tiled=True)
    return (layer_out, hessian)


def solution(mesh):
    in_plane = mesh.shape["expert"] == PLANES * PLANE and mesh.shape["hidden"] == 2
    return jax.shard_map(
        kernel_body if in_plane else body,
        mesh=mesh,
        in_specs=(
            P("expert", "hidden"),
            P("expert", None),
            P("expert", None),
            P("expert", None, "hidden", None),
            P("expert", None, "hidden"),
        ),
        out_specs=(P("expert", "hidden"), P("expert", "hidden", None)),
        check_vma=False,
    )
```

```python
import jax
import jax.numpy as jnp
from jax import lax
from jax.experimental import pallas as pl
from jax.experimental.pallas import tpu as pltpu
from jax.sharding import PartitionSpec as P

PLANES = 4
PLANE = 4
FIRST = (1, 2, 1, 2)
SECOND = (2, 0, 3, 1)
THIRD = (3, 3, 0, 0)
NAMES = ("zd", "zr", "xr", "yr", "dx", "dy", "c0", "c1", "c2", "c3", "tz", "tx", "ty", "td", "hr",
         "ax", "ay", "bx0", "bx1", "by0", "by1", "z00", "z01", "z10", "z11")
SENDS = 128


def pick(values, z):
    chosen = jnp.int32(values[0])
    for place in range(1, len(values)):
        chosen = jnp.where(z == place, jnp.int32(values[place]), chosen)
    return chosen


def layer_kernel(tokens, ids, weights, gate_up, down, out, hess_out,
                 feats, shares, hid, part, got_ax, got_ay, got_bx, got_by, got_z,
                 w_gate, w_down, hess, send_sem, recv_sem, load_sem):
    rows, width = tokens.shape
    half = rows // 2
    units = hid.shape[-1]
    me = lax.axis_index("expert")
    c = lax.axis_index("hidden")
    z, j = me // PLANE, me % PLANE
    xj, yj, dj = j + 1 - 2 * (j % 2), (j + 2) % PLANE, PLANE - 1 - j
    ex, ey = z * PLANE + xj, z * PLANE + yj
    at_end = z % (PLANES - 1) == 0
    inside = z % (PLANES - 1) != 0
    a1, a2, a3 = pick(FIRST, z), pick(SECOND, z), pick(THIRD, z)
    lo, hi = pl.ds(0, half), pl.ds(half, half)
    all_rows = pl.ds(0, rows)
    started = []

    load_gate = pltpu.make_async_copy(gate_up.at[0], w_gate, load_sem.at[0])
    load_down = pltpu.make_async_copy(down.at[0], w_down, load_sem.at[1])
    load_gate.start()
    load_down.start()

    def sem(name, k):
        return recv_sem.at[NAMES.index(name) * PLANES + k]

    def send(src, dst, to, name, k, core=None, when=None):
        copy = pltpu.make_async_remote_copy(
            src_ref=src, dst_ref=dst, send_sem=send_sem.at[len(started)], recv_sem=sem(name, k),
            device_id=(to, c if core is None else core), device_id_type=pl.DeviceIdType.MESH)
        started.append((copy, when))
        if when is None:
            copy.start()
        else:
            pl.when(when)(copy.start)

    def landed(dst, name, k):
        pltpu.make_async_remote_copy(
            src_ref=dst, dst_ref=dst, send_sem=send_sem.at[0], recv_sem=sem(name, k),
            device_id=(me, 1 - c), device_id_type=pl.DeviceIdType.MESH).wait_recv()

    def block(k, q, part_rows=all_rows):
        return feats.at[c, k, q, part_rows]

    def across(k, q, name):
        send(block(k, q), block(k, q), me, name, k, core=1 - c)

    def sides(k):
        for to, name, tname in ((ex, "xr", "tx"), (ey, "yr", "ty")):
            send(shares.at[k, j], shares.at[k, j], to, tname, k)
            send(block(k, j), block(k, j), to, name, k)

    def column(k):
        landed(shares.at[k, j], "tz", k)
        landed(block(k, j), "zr", k)
        to = jnp.where(k < z, me + PLANE, me - PLANE)
        send(shares.at[k, j], shares.at[k, j], to, "tz", k, when=inside)
        send(block(k, j), block(k, j), to, "zr", k, when=inside)
        across(k, j, "c0")

    def relay(k, halves, when=None):
        landed(shares.at[k, yj], "ty", k)
        landed(shares.at[k, xj], "tx", k)
        send(shares.at[k, yj], shares.at[k, yj], ex, "td", k)
        landed(block(k, yj), "yr", k)
        if halves:
            send(block(k, yj, lo), block(k, yj, lo), ex, "dx", k, when=when)
        across(k, yj, "c2")
        landed(block(k, xj), "xr", k)
        if halves:
            send(block(k, xj, hi), block(k, xj, hi), ey, "dy", k, when=when)
        across(k, xj, "c1")

    def corner_own():
        landed(shares.at[z, dj], "td", z)
        landed(block(z, dj, lo), "dx", z)
        landed(block(z, dj, hi), "dy", z)
        for to, when in ((me - PLANE, z > 0), (me + PLANE, z < PLANES - 1)):
            send(block(z, dj), block(z, dj), to, "zd", z, when=when)
        across(z, dj, "c3")

    def corner_near(k):
        landed(shares.at[k, dj], "td", k)
        landed(block(k, dj), "zd", k)
        to = jnp.where(k < z, me + PLANE, me - PLANE)
        send(block(k, dj), block(k, dj), to, "zd", k, when=inside)
        across(k, dj, "c3")

    def corner_far(k):
        landed(shares.at[k, dj], "td", k)

        @pl.when(at_end)
        def _():
            landed(block(k, dj, lo), "dx", k)
            landed(block(k, dj, hi), "dy", k)

        @pl.when(inside)
        def _():
            landed(block(k, dj), "zd", k)

        across(k, dj, "c3")

    def other_core(k):
        for q, name in ((j, "c0"), (xj, "c1"), (yj, "c2"), (dj, "c3")):
            landed(feats.at[1 - c, k, q], name, k)

    def share_table():
        experts, lanes = shares.shape[2:]
        share = weights[...] / jnp.sum(weights[...], axis=0, keepdims=True)
        expert = lax.broadcasted_iota(jnp.int32, (experts, rows), 0)
        dense = jnp.zeros((experts, rows), jnp.float32)
        for q in range(ids.shape[0]):
            dense = dense + jnp.where(ids[q:q + 1, :] == expert, share[q:q + 1, :], 0.0)
        shares[z, j] = jnp.concatenate([dense, jnp.zeros((experts, lanes - rows), jnp.float32)], axis=1)

    def my_share(k):
        lanes = shares.shape[-1]
        lane = lax.broadcasted_iota(jnp.int32, (rows, lanes), 1)
        line = lax.broadcasted_iota(jnp.int32, (rows, lanes), 0)
        columns = []
        for q in range(PLANE):
            values = jnp.broadcast_to(shares[k, q, pl.ds(me, 1), :], (rows, lanes))
            columns.append(jnp.sum(jnp.where(lane == line, values, 0.0), axis=1, keepdims=True))
        return jnp.concatenate(columns, axis=0)

    def up_side(k, w):
        total = None
        for side in range(2):
            x = feats[side, k].reshape(PLANE * rows, width)
            wg = w_gate[:, :, side * width:(side + 1) * width].reshape(2 * units, width)
            term = lax.dot_general(x, wg, (((1,), (1,)), ((), ())), preferred_element_type=jnp.float32)
            total = term if total is None else total + term
        gate, upward = total[:, :units], total[:, units:]
        value = gate / (1.0 + jnp.exp(-gate)) * upward
        hid[c, k] = jnp.where(w > 0, value, 0.0).astype(jnp.bfloat16)
        send(hid.at[c, k], hid.at[c, k], me, "hr", k, core=1 - c)

    def down_side(k, w, first):
        landed(hid.at[1 - c, k], "hr", k)
        mine = hid[c, k]
        for side in range(2):
            cols = slice(side * units, (side + 1) * units)
            gram = lax.dot_general(mine, hid[side, k], (((0,), (0,)), ((), ())),
                                   preferred_element_type=jnp.float32)
            hess[:, cols] = gram if first else hess[:, cols] + gram
        step = 512
        for start in range(0, width, step):
            cols = slice(start, start + step)
            o = jnp.dot(hid[0, k], w_down[:units, cols], preferred_element_type=jnp.float32)
            o = o + jnp.dot(hid[1, k], w_down[units:, cols], preferred_element_type=jnp.float32)
            part[k, :, :, cols] = (o * w).astype(jnp.bfloat16).reshape(PLANE, rows, step)

    def give(k):
        send(part.at[k, dj, lo], got_ax.at[k], ex, "ax", k)
        send(part.at[k, dj, hi], got_ay.at[k], ey, "ay", k)
        send(part.at[k, xj, lo], got_bx.at[k, lo], ex, "bx0", k)
        send(part.at[k, yj, hi], got_by.at[k, hi], ey, "by1", k)

    def add_up(*terms):
        total = terms[0].astype(jnp.float32)
        for term in terms[1:]:
            total = total + term.astype(jnp.float32)
        return total.astype(jnp.bfloat16)

    def pass_on(k):
        landed(got_ax.at[k], "ax", k)
        part[k, yj, lo] = add_up(part[k, yj, lo], got_ax[k])
        send(part.at[k, yj, lo], got_by.at[k, lo], ey, "by0", k)
        landed(got_ay.at[k], "ay", k)
        part[k, xj, hi] = add_up(part[k, xj, hi], got_ay[k])
        send(part.at[k, xj, hi], got_bx.at[k, hi], ex, "bx1", k)

    def plane_done(k):
        landed(got_bx.at[k, lo], "bx0", k)
        landed(got_bx.at[k, hi], "bx1", k)
        landed(got_by.at[k, lo], "by0", k)
        landed(got_by.at[k, hi], "by1", k)

    pieces = [slice(0, width // 2), slice(width // 2, width)]

    def z_sem(slot, k, p):
        return recv_sem.at[(NAMES.index("z00") + 2 * slot + p) * PLANES + k]

    def z_copies(k, when):
        slot = jnp.where(k > z, 0, 1)
        to = jnp.where(k > z, me + PLANE, me - PLANE)
        copies = []
        for p, cols in enumerate(pieces):
            copy = pltpu.make_async_remote_copy(
                src_ref=part.at[k, j, :, cols], dst_ref=got_z.at[slot, k, :, cols],
                send_sem=send_sem.at[len(started)], recv_sem=z_sem(slot, k, p),
                device_id=(to, c), device_id_type=pl.DeviceIdType.MESH)
            started.append((copy, when))
            copies.append(copy)
        return copies, slot

    def z_landed(slot, k, p):
        dst = got_z.at[slot, k, :, pieces[p]]
        pltpu.make_async_remote_copy(
            src_ref=dst, dst_ref=dst, send_sem=send_sem.at[0], recv_sem=z_sem(slot, k, p),
            device_id=(me, 1 - c), device_id_type=pl.DeviceIdType.MESH).wait_recv()

    def chain_end(k):
        copies, _ = z_copies(k, at_end)

        @pl.when(at_end)
        def _():
            plane_done(k)
            for copy, cols in zip(copies, pieces):
                part[k, j, :, cols] = add_up(part[k, j, :, cols], got_bx[k, :, cols], got_by[k, :, cols])
                copy.start()

    def chain_inside(k):
        copies, slot = z_copies(k, inside)

        @pl.when(inside)
        def _():
            plane_done(k)
            for p, cols in enumerate(pieces):
                z_landed(slot, k, p)
                part[k, j, :, cols] = add_up(part[k, j, :, cols], got_bx[k, :, cols], got_by[k, :, cols],
                                             got_z[slot, k, :, cols])
                copies[p].start()

    barrier = pltpu.get_barrier_semaphore()

    def greet(to, core):
        pl.semaphore_signal(barrier, inc=1, device_id=(to, core), device_id_type=pl.DeviceIdType.MESH)

    greet(me, 1 - c)
    greet(ex, c)
    greet(ey, c)
    pl.when(z > 0)(lambda: greet(me - PLANE, c))
    pl.when(z < PLANES - 1)(lambda: greet(me + PLANE, c))
    feats[c, z, j] = tokens[...]
    pl.when(at_end)(lambda: pl.semaphore_wait(barrier, 4))
    pl.when(inside)(lambda: pl.semaphore_wait(barrier, 5))

    for to, when in ((me - PLANE, z > 0), (me + PLANE, z < PLANES - 1)):
        send(block(z, j), block(z, j), to, "zr", z, when=when)
    send(block(z, j), block(z, j), ex, "xr", z)
    send(block(z, j), block(z, j), ey, "yr", z)
    across(z, j, "c0")
    share_table()
    for to, when in ((me - PLANE, z > 0), (me + PLANE, z < PLANES - 1)):
        send(shares.at[z, j], shares.at[z, j], to, "tz", z, when=when)
    send(shares.at[z, j], shares.at[z, j], ex, "tx", z)
    send(shares.at[z, j], shares.at[z, j], ey, "ty", z)
    column(a1)
    sides(a1)
    relay(z, True)
    column(a2)
    corner_own()
    relay(a1, False)
    column(a3)
    sides(a3)
    sides(a2)

    load_gate.wait()
    load_down.wait()

    def up_round(k):
        other_core(k)
        w = my_share(k)
        up_side(k, w)
        return w, jnp.sum((w > 0).astype(jnp.float32), axis=0, keepdims=True)

    w, count = up_round(z)
    corner_near(a1)
    down_side(z, w, True)
    relay(a3, True, when=at_end)

    w, hits = up_round(a1)
    count = count + hits
    relay(a2, False)
    corner_near(a2)
    down_side(a1, w, False)
    give(a1)
    corner_far(a3)

    w, hits = up_round(a3)
    count = count + hits
    down_side(a3, w, False)
    give(a3)
    pass_on(a1)

    w, hits = up_round(a2)
    count = count + hits
    down_side(a2, w, False)
    give(a2)

    pass_on(a3)
    chain_end(a1)
    pass_on(a2)
    give(z)
    hess[...] = hess[...] * (2.0 / count)
    store = pltpu.make_async_copy(hess, hess_out.at[0], load_sem.at[2])
    store.start()
    chain_end(a3)
    chain_inside(a3)
    pass_on(z)
    chain_end(a2)
    chain_inside(pick((0, 0, 3, 0), z))
    chain_inside(pick((0, 2, 1, 0), z))
    plane_done(z)

    @pl.when(at_end)
    def _():
        slot = jnp.where(z > 0, 0, 1)
        for p, cols in enumerate(pieces):
            z_landed(slot, z, p)
            out[:, cols] = add_up(part[z, j, :, cols], got_bx[z, :, cols], got_by[z, :, cols],
                                  got_z[slot, z, :, cols])

    @pl.when(inside)
    def _():
        for p, cols in enumerate(pieces):
            z_landed(0, z, p)
            z_landed(1, z, p)
            out[:, cols] = add_up(part[z, j, :, cols], got_bx[z, :, cols], got_by[z, :, cols],
                                  got_z[0, z, :, cols], got_z[1, z, :, cols])

    store.wait()
    for copy, when in started:
        if when is None:
            copy.wait_send()
        else:
            pl.when(when)(copy.wait_send)


def results_kernel(out_in, hess_in, out, hess, out_held, hess_held, in_sem, out_sem):
    pairs = ((hess_in, hess_held, hess), (out_in, out_held, out))
    loads = [pltpu.make_async_copy(src, held, in_sem.at[n]) for n, (src, held, _) in enumerate(pairs)]
    stores = [pltpu.make_async_copy(held, dst, out_sem.at[n]) for n, (_, held, dst) in enumerate(pairs)]
    for load in loads:
        load.start()
    for load, store in zip(loads, stores):
        load.wait()
        store.start()
    for store in stores:
        store.wait()


def kernel_body(tokens, route_ids, route_weights, gate_up, down_proj):
    rows, width = tokens.shape
    experts = lax.axis_size("expert")
    units = gate_up.shape[2]
    lanes = 128
    bf, f32 = jnp.bfloat16, jnp.float32
    out, hess = pl.pallas_call(
        layer_kernel,
        out_shape=(
            jax.ShapeDtypeStruct((rows, width), bf),
            jax.ShapeDtypeStruct((1, units, 2 * units), f32),
        ),
        in_specs=[pl.BlockSpec(memory_space=pltpu.VMEM)] * 3 + [pl.BlockSpec(memory_space=pl.ANY)] * 2,
        out_specs=(pl.BlockSpec(memory_space=pltpu.VMEM), pl.BlockSpec(memory_space=pl.ANY)),
        scratch_shapes=[
            pltpu.VMEM((2, PLANES, PLANE, rows, width), bf),
            pltpu.VMEM((PLANES, PLANE, experts, lanes), f32),
            pltpu.VMEM((2, PLANES, PLANE * rows, units), bf),
            pltpu.VMEM((PLANES, PLANE, rows, width), bf),
            pltpu.VMEM((PLANES, rows // 2, width), bf),
            pltpu.VMEM((PLANES, rows // 2, width), bf),
            pltpu.VMEM((PLANES, rows, width), bf),
            pltpu.VMEM((PLANES, rows, width), bf),
            pltpu.VMEM((2, PLANES, rows, width), bf),
            pltpu.VMEM(gate_up.shape[1:], bf),
            pltpu.VMEM(down_proj.shape[1:], bf),
            pltpu.VMEM((units, 2 * units), f32),
            pltpu.SemaphoreType.DMA((SENDS,)),
            pltpu.SemaphoreType.DMA((len(NAMES) * PLANES,)),
            pltpu.SemaphoreType.DMA((3,)),
        ],
        compiler_params=pltpu.CompilerParams(
            collective_id=0, has_side_effects=True, vmem_limit_bytes=56 * 1024 * 1024
        ),
        name="moe_layer",
    )(tokens, route_ids.T, route_weights.T, gate_up, down_proj)
    return pl.pallas_call(
        results_kernel,
        out_shape=(jax.ShapeDtypeStruct(out.shape, out.dtype), jax.ShapeDtypeStruct(hess.shape, hess.dtype)),
        in_specs=[pl.BlockSpec(memory_space=pl.ANY)] * 2,
        out_specs=(pl.BlockSpec(memory_space=pl.ANY),) * 2,
        scratch_shapes=[pltpu.VMEM(out.shape, out.dtype), pltpu.VMEM(hess.shape, hess.dtype),
                        pltpu.SemaphoreType.DMA((2,)), pltpu.SemaphoreType.DMA((2,))],
        compiler_params=pltpu.CompilerParams(vmem_limit_bytes=56 * 1024 * 1024),
        name="results",
    )(out, hess)


def body(tokens, route_ids, route_weights, gate_up, down_proj):
    local_experts = gate_up.shape[0]
    all_experts = local_experts * lax.axis_size("expert")
    share = route_weights / jnp.sum(route_weights, axis=1, keepdims=True)
    hit = route_ids[:, :, None] == jnp.arange(all_experts, dtype=jnp.int32)[None, None, :]
    table = jnp.sum(jnp.where(hit, share[:, :, None], 0.0), axis=1)
    table = lax.all_gather(table.T, "expert", axis=1, tiled=True)
    mine = lax.dynamic_slice_in_dim(
        table, lax.axis_index("expert") * local_experts, local_experts, axis=0
    )
    features = lax.all_gather(tokens, "expert", axis=0, tiled=True)
    features = lax.all_gather(features, "hidden", axis=1, tiled=True)
    routed = jnp.sum((mine > 0).astype(jnp.float32), axis=1)
    gate = jnp.einsum("td,efd->etf", features, gate_up[:, 0], preferred_element_type=jnp.float32)
    upward = jnp.einsum("td,efd->etf", features, gate_up[:, 1], preferred_element_type=jnp.float32)
    hidden = jnp.where((mine > 0)[:, :, None], jax.nn.silu(gate) * upward, 0.0).astype(jnp.bfloat16)
    rows = lax.all_gather(hidden, "hidden", axis=2, tiled=True)
    columns = jnp.einsum("etf,etg->efg", hidden, rows, preferred_element_type=jnp.float32)
    hessian = columns * (2.0 / routed)[:, None, None]
    out = jnp.einsum("etg,egd->etd", rows, down_proj, preferred_element_type=jnp.float32)
    out = jnp.sum(out * mine[:, :, None], axis=0).astype(jnp.bfloat16)
    layer_out = lax.psum_scatter(out, "expert", scatter_dimension=0, tiled=True)
    return (layer_out, hessian)


def solution(mesh):
    in_plane = mesh.shape["expert"] == PLANES * PLANE and mesh.shape["hidden"] == 2
    return jax.shard_map(
        kernel_body if in_plane else body,
        mesh=mesh,
        in_specs=(
            P("expert", "hidden"),
            P("expert", None),
            P("expert", None),
            P("expert", None, "hidden", None),
            P("expert", None, "hidden"),
        ),
        out_specs=(P("expert", "hidden"), P("expert", "hidden", None)),
        check_vma=False,
    )
```
